32 devices in a mesh: tile: 16 (over z, x, core), build: 2 (over y).
Axes of the slice: x: 2, y: 2, z: 4, core: 2. Of those that a mesh axis runs over, the one named last changes fastest.
Arguments:
- loads: float32 [8, 3, 128, 128], P('build', None, 'tile'), may hold values from -4 to 4
- guess: float32 [8, 3, 128, 128], P('build', None, 'tile'), may hold values from -0.6 to 0.6
- material: int32 [8, 128, 128], P('build', 'tile'), may hold values from 0 to 1
- clamped: int32 [8, 128, 128], P('build', 'tile'), may hold values 0 or 1
- moduli: float32 [2], replicated, may hold values from 0.3 to 3
Outputs:
- distortion: float32 [8, 3, 128, 128], P('build', None, 'tile')
- imbalance: float32 [8, 3, 128, 128], P('build', None, 'tile')
The draws below stay inside these ranges and needn't reach their ends.
Inputs may be any that keep to these rules, and one draw needn't show every extreme that they name: `material`: 0 marks a support element, 1 a part element.
All inputs are finite; a program needn't handle non-finite values. No bound on the sum of `clamped` on one device may be relied on, other than what follows from the above.
Results may differ from the reference program's by a relative error of at most 0.0003.
Values sent between devices are 32-bit elements; how exact they have to be, the bound alone decides.
A program may use at most 64 MiB of HBM per device.

```python
import math
import jax
import jax.numpy as jnp
import numpy as np
from jax import lax

NY = 128
SWEEPS = 2
NZ = 8
NX = 128


def draw_loads(key, part):
    shape_all = (NZ, 3, NX, NY)
    base = jax.random.normal(jax.random.fold_in(key, 11), shape_all, jnp.float32)
    return jnp.clip(base, -4.0, 4.0)


def with_ends(values, key, low, high):
    extent = values.shape
    spot = [jax.random.randint(jax.random.fold_in(key, axis), (), 0, extent[axis]) for axis in range(len(extent))]
    values = values.at[tuple(spot)].set(low)
    longest = extent.index(max(extent))
    spot[longest] = (spot[longest] + 1) % extent[longest]
    return values.at[tuple(spot)].set(high)


def shard_levels(key, extent, split, low, high):
    level, own = 1.0, jax.random.fold_in(key, 6)
    for axis_at, parts in split:
        draws = jnp.exp(jax.random.uniform(jax.random.fold_in(own, axis_at), (parts,), jnp.float32, low / len(split), high / len(split)))
        level = level * jnp.repeat(draws, extent[axis_at] // parts).reshape([-1 if axis == axis_at else 1 for axis in range(len(extent))])
    return level


def scatter_about(key, extent, spread, bound, split=(), kind=jnp.bfloat16):
    gain = shard_levels(key, extent, split, -0.22, 0.18) if split else 1.0
    result = jax.random.normal(key, extent, jnp.float32) * spread * gain
    return jnp.minimum(jnp.maximum(result, -bound), bound).astype(kind)


def setup_inputs(seed: int = 0) -> dict:
    splits = jax.random.split(jax.random.key(seed), 6)
    return {
        "loads": draw_loads(jax.random.fold_in(splits[5], 71), 0),
        "guess": scatter_about(splits[1], (NZ, 3, NX, NY), 0.1, 0.6, ((0, 2), (2, 16)), jnp.float32),
        "material": with_ends(jax.random.randint(splits[2], (NZ, NX, NY), 0, 2), jax.random.fold_in(splits[2], 1), 0, 1).astype(jnp.int32),
        "clamped": with_ends((jax.random.randint(splits[3], (NZ, NX, NY), 0, 64) < 1).astype(jnp.int32), jax.random.fold_in(splits[3], 1), 0, 1),
        "moduli": jnp.clip(jnp.exp(jax.random.uniform(splits[4], (2,), jnp.float32, math.log(0.3), math.log(3.0))), 0.3, 3.0),
    }


relax_shifts = (0.0, 0.05, 0.2)
relax_weights = (0.5, 0.3, 0.2)

def element_matrix():
    spacing = np.array([1.0, 8.0, 8.0])
    poisson = 0.3
    lame_first = poisson / ((1.0 + poisson) * (1.0 - 2.0 * poisson))
    lame_second = 0.5 / (1.0 + poisson)
    elastic = np.zeros((6, 6))
    elastic[:3, :3] = lame_first
    for entry in range(3):
        elastic[entry, entry] += 2.0 * lame_second
        elastic[3 + entry, 3 + entry] = lame_second
    points = (0.5 - 0.5 / math.sqrt(3.0), 0.5 + 0.5 / math.sqrt(3.0))
    matrix = np.zeros((24, 24))
    volume = float(np.prod(spacing)) / 8.0
    for point_z in points:
        for point_x in points:
            for point_y in points:
                position = (point_z, point_x, point_y)
                strain = np.zeros((6, 24))
                for corner in range(8):
                    upper_side = (corner >> 2 & 1, corner >> 1 & 1, corner & 1)
                    values = [position[direction] if upper_side[direction] else 1.0 - position[direction] for direction in range(3)]
                    slopes = [(1.0 if upper_side[direction] else -1.0) / spacing[direction] for direction in range(3)]
                    gradient = [slopes[0] * values[1] * values[2], values[0] * slopes[1] * values[2], values[0] * values[1] * slopes[2]]
                    column = 3 * corner
                    strain[0, column] = gradient[0]
                    strain[1, column + 1] = gradient[1]
                    strain[2, column + 2] = gradient[2]
                    strain[3, column] = gradient[1]
                    strain[3, column + 1] = gradient[0]
                    strain[4, column + 1] = gradient[2]
                    strain[4, column + 2] = gradient[1]
                    strain[5, column] = gradient[2]
                    strain[5, column + 2] = gradient[0]
                matrix += strain.T @ elastic @ strain * volume
    largest = 0.0
    for entry in range(24):
        largest = largest if largest >= float(matrix[entry, entry]) else float(matrix[entry, entry])
    return matrix / largest

def corner_steps(corner):
    return (corner >> 2 & 1, corner >> 1 & 1, corner & 1)

def element_forces(extended, moduli_ext, stiffness):
    depth = extended.shape[0] - 2
    width = extended.shape[2] - 2
    length = extended.shape[3] - 2
    pieces = []
    for corner in range(8):
        step_z, step_x, step_y = corner_steps(corner)
        pieces.append(extended[step_z:step_z + depth + 1, :, step_x:step_x + width + 1, step_y:step_y + length + 1])
    stacked = jnp.concatenate(pieces, axis=1)
    forces = jnp.einsum('ij,zjxy->zixy', stiffness, stacked, precision=lax.Precision.HIGHEST)
    forces = forces * moduli_ext[:, None]
    summed = jnp.zeros((depth, 3, width, length), jnp.float32)
    for corner in range(8):
        step_z, step_x, step_y = corner_steps(corner)
        summed = summed + forces[1 - step_z:1 - step_z + depth, 3 * corner:3 * corner + 3, 1 - step_x:1 - step_x + width, 1 - step_y:1 - step_y + length]
    return summed

def line_blocks(moduli_ext, free, stiffness):
    depth, width, length = free.shape
    diagonal = jnp.zeros((depth, 3, 3, width, length), jnp.float32)
    for corner in range(8):
        step_z, step_x, step_y = corner_steps(corner)
        sub_block = stiffness[3 * corner:3 * corner + 3, 3 * corner:3 * corner + 3]
        weight = moduli_ext[1 - step_z:1 - step_z + depth, 1 - step_x:1 - step_x + width, 1 - step_y:1 - step_y + length]
        diagonal = diagonal + sub_block[None, :, :, None, None] * weight[:, None, None]
    upper_blocks = jnp.zeros((depth + 1, 3, 3, width, length), jnp.float32)
    for corner in range(4):
        step_x, step_y = (corner >> 1, corner & 1)
        sub_block = stiffness[3 * corner:3 * corner + 3, 3 * corner + 12:3 * corner + 15]
        weight = moduli_ext[:, 1 - step_x:1 - step_x + width, 1 - step_y:1 - step_y + length]
        upper_blocks = upper_blocks + sub_block[None, :, :, None, None] * weight[:, None, None]
    identity = jnp.eye(3, dtype=jnp.float32)[None, :, :, None, None]
    free_rows = free[:, None, None]
    diagonal = free_rows * diagonal + (1.0 - free_rows) * identity
    above = free_rows * upper_blocks[1:]
    below = free_rows * jnp.swapaxes(upper_blocks[:-1], 1, 2)
    return (diagonal, below, above)

def apply(matrix, other):
    extra = other.ndim - matrix.ndim + 1
    summed = None
    for entry in range(3):
        left = matrix[:, entry]
        left = left.reshape(left.shape[:1] + (1,) * extra + left.shape[1:])
        product = left * other[entry]
        summed = product if summed is None else summed + product
    return summed

def invert(matrix):
    entries = [[matrix[row_index, col_index] for col_index in range(3)] for row_index in range(3)]

    def cofactor(row_index, col_index):
        return entries[(row_index + 1) % 3][(col_index + 1) % 3] * entries[(row_index + 2) % 3][(col_index + 2) % 3] - entries[(row_index + 1) % 3][(col_index + 2) % 3] * entries[(row_index + 2) % 3][(col_index + 1) % 3]
    determinant = entries[0][0] * cofactor(0, 0) + entries[0][1] * cofactor(0, 1) + entries[0][2] * cofactor(0, 2)
    rows_out = [jnp.stack([cofactor(col_index, row_index) / determinant for col_index in range(3)]) for row_index in range(3)]
    return jnp.stack(rows_out)

def factorize(scaled, below, above):

    def eliminate(previous, inputs):
        pivot_block, below_block, above_block = inputs
        inverse = invert(pivot_block - apply(below_block, previous))
        couple = apply(inverse, above_block)
        return (couple, (inverse, couple))
    initial = jnp.zeros(scaled.shape[1:], jnp.float32)
    unused, (inverses, couples) = lax.scan(eliminate, initial, (scaled, below, above))
    return (inverses, couples)

def substitute(inverses, couples, below, right_side):

    def forward(previous, inputs):
        inverse, below_block, right_block = inputs
        current = apply(inverse, right_block - apply(below_block, previous))
        return (current, current)
    initial = jnp.zeros(right_side.shape[1:], jnp.float32)
    unused, eliminated = lax.scan(forward, initial, (inverses, below, right_side))

    def backward(following, inputs):
        couple, current = inputs
        solved = current - apply(couple, following)
        return (solved, solved)
    unused, solution = lax.scan(backward, initial, (couples, eliminated), reverse=True)
    return solution

def reference(loads, guess, material, clamped, moduli):
    stiffness = jnp.asarray(element_matrix(), jnp.float32)
    free = (1 - clamped).astype(jnp.float32)
    modulus = jnp.where(material == 1, moduli[1], moduli[0]).astype(jnp.float32)
    moduli_ext = jnp.pad(modulus, ((1, 0), (1, 0), (1, 0)))
    diagonal, below, above = line_blocks(moduli_ext, free, stiffness)

    def residual_of(field):
        extended = jnp.pad(field, ((1, 1), (0, 0), (1, 1), (1, 1)))
        return free[:, None] * (loads - element_forces(extended, moduli_ext, stiffness))
    displacement = guess
    for sweep_index in range(SWEEPS):
        residual = residual_of(displacement)
        update = jnp.zeros_like(displacement)
        for shift_value, weight in zip(relax_shifts, relax_weights):
            inverses, couples = factorize((1.0 + shift_value) * diagonal, below, above)
            update = update + weight * substitute(inverses, couples, below, residual)
        displacement = displacement + update
    return (displacement, residual_of(displacement))
```

```python
import functools
import math

import jax
import jax.numpy as jnp
import numpy as np
from jax import lax
from jax.experimental import pallas as pl
from jax.experimental.pallas import tpu as pltpu
from jax.sharding import PartitionSpec as P

SWEEPS = 2
MESH = pl.DeviceIdType.MESH

relax_shifts = (0.0, 0.05, 0.2)
relax_weights = (0.5, 0.3, 0.2)


def element_matrix():
    spacing = np.array([1.0, 8.0, 8.0])
    poisson = 0.3
    lame_first = poisson / ((1.0 + poisson) * (1.0 - 2.0 * poisson))
    lame_second = 0.5 / (1.0 + poisson)
    elastic = np.zeros((6, 6))
    elastic[:3, :3] = lame_first
    for entry in range(3):
        elastic[entry, entry] += 2.0 * lame_second
        elastic[3 + entry, 3 + entry] = lame_second
    points = (0.5 - 0.5 / math.sqrt(3.0), 0.5 + 0.5 / math.sqrt(3.0))
    matrix = np.zeros((24, 24))
    volume = float(np.prod(spacing)) / 8.0
    for point_z in points:
        for point_x in points:
            for point_y in points:
                position = (point_z, point_x, point_y)
                strain = np.zeros((6, 24))
                for corner in range(8):
                    upper_side = (corner >> 2 & 1, corner >> 1 & 1, corner & 1)
                    values = [
                        position[direction] if upper_side[direction] else 1.0 - position[direction]
                        for direction in range(3)
                    ]
                    slopes = [
                        (1.0 if upper_side[direction] else -1.0) / spacing[direction]
                        for direction in range(3)
                    ]
                    gradient = [
                        slopes[0] * values[1] * values[2],
                        values[0] * slopes[1] * values[2],
                        values[0] * values[1] * slopes[2],
                    ]
                    column = 3 * corner
                    strain[0, column] = gradient[0]
                    strain[1, column + 1] = gradient[1]
                    strain[2, column + 2] = gradient[2]
                    strain[3, column] = gradient[1]
                    strain[3, column + 1] = gradient[0]
                    strain[4, column + 1] = gradient[2]
                    strain[4, column + 2] = gradient[1]
                    strain[5, column] = gradient[2]
                    strain[5, column + 2] = gradient[0]
                matrix += strain.T @ elastic @ strain * volume
    largest = 0.0
    for entry in range(24):
        largest = largest if largest >= float(matrix[entry, entry]) else float(matrix[entry, entry])
    return matrix / largest


def parity_blocks():
    pair = np.array([[1.0, 1.0], [-1.0, 1.0]])
    modes = np.kron(np.kron(np.kron(pair, pair), pair), np.eye(3))
    matrix = modes @ element_matrix() @ modes.T / 64.0
    terms = {}
    for parity in range(8):
        index = [3 * (parity ^ (4 >> comp)) + comp for comp in range(3)]
        for row in index:
            terms[divmod(row, 3)] = [
                (divmod(col, 3), float(matrix[row, col]))
                for col in index
                if abs(matrix[row, col]) > 1e-12
            ]
    return terms


def total(values):
    values = list(values)
    while len(values) > 1:
        paired = [a + b for a, b in zip(values[::2], values[1::2])]
        values = paired + values[len(values) - len(values) % 2 :]
    return values[0]


def kernel(
    layers, tiles, loads, guess, material, clamped, moduli, distortion, imbalance,
    mat_buf, cl_buf, u0_buf, r_buf, m_buf, free_buf, du_buf, fac_buf, y_buf,
    send_sem, recv_sem, u_send_sem, u_recv_sem,
):
    depth, comps, rows, lanes = loads.shape
    height = depth * layers
    wide = 2 * rows
    build = lax.axis_index("build")
    tile = lax.axis_index("tile")
    base = build * depth
    has = {-1: tile > 0, 0: None, 1: tile < tiles - 1}
    z_has = {-1: build > 0, 0: None, 1: build < layers - 1}
    stiff = element_matrix()
    terms = parity_blocks()

    def when(condition, run):
        if condition is None:
            run()
        else:
            pl.when(condition)(run)

    halo = pl.ds(rows, rows)
    mat_buf[:, halo] = jnp.zeros((height, rows, lanes), jnp.int32)
    cl_buf[:, halo] = jnp.ones((height, rows, lanes), jnp.int32)
    u0_buf[...] = jnp.zeros(u0_buf.shape, jnp.float32)
    r_buf[:, :, halo] = jnp.zeros((height, comps, rows, lanes), jnp.float32)

    barrier = pltpu.get_barrier_semaphore()
    peers = [(side, offset) for offset in range(layers) for side in (0, 1, -1) if side or offset]

    def device(side, offset):
        return {"tile": tile + side, "build": lax.rem(build + offset, layers)}

    for side, offset in peers:
        def greet(side=side, offset=offset):
            pl.semaphore_signal(barrier, inc=1, device_id=device(side, offset), device_id_type=MESH)
        when(has[side], greet)
    sides = has[-1].astype(jnp.int32) + has[1].astype(jnp.int32)
    pl.semaphore_wait(barrier, layers - 1 + layers * sides)

    def spans(side, before, after):
        if side == 0:
            return pl.ds(0, rows), pl.ds(0, rows)
        if side == 1:
            return pl.ds(rows - before, before), pl.ds(wide - before, before)
        return pl.ds(0, after), pl.ds(rows, after)

    def slab_copy(kind, side, offset, source_build):
        before, after = ((3, 2), (2, 2), (2, 2))[kind]
        take, put = spans(side, before, after)
        here = pl.ds(base, depth)
        there = pl.ds(source_build * depth, depth)
        if kind == 2:
            source, target = r_buf.at[here, :, take], r_buf.at[there, :, put]
        else:
            operand, buffer = ((material, mat_buf), (clamped, cl_buf))[kind]
            source, target = operand.at[:, take], buffer.at[there, put]
        return pltpu.make_async_remote_copy(
            src_ref=source, dst_ref=target,
            send_sem=send_sem.at[kind, side + 1, offset],
            recv_sem=recv_sem.at[kind, side + 1, offset],
            device_id=device(side, offset), device_id_type=MESH,
        )

    def each_slab(kind, act):
        for side, offset in peers:
            def run(side=side, offset=offset):
                act(kind, side, offset)
            when(has[-side if act is slab_arrive else side] if side else None, run)

    def slab_start(kind, side, offset):
        slab_copy(kind, side, offset, build).start()

    def slab_sent(kind, side, offset):
        slab_copy(kind, side, offset, build).wait_send()

    def slab_arrive(kind, side, offset):
        slab_copy(kind, side, offset, lax.rem(build + layers - offset, layers)).wait_recv()

    def u0_copy(side, step):
        take, put = spans(side, 1, 1)
        from_z, to_z = {0: (pl.ds(0, depth), pl.ds(1, depth)),
                        1: (pl.ds(depth - 1, 1), pl.ds(0, 1)),
                        -1: (pl.ds(0, 1), pl.ds(depth + 1, 1))}[step]
        return pltpu.make_async_remote_copy(
            src_ref=guess.at[from_z, :, take], dst_ref=u0_buf.at[to_z, :, put],
            send_sem=u_send_sem.at[step + 1, side + 1], recv_sem=u_recv_sem.at[step + 1, side + 1],
            device_id={"tile": tile + side, "build": build + step}, device_id_type=MESH,
        )

    def each_u0(act, sign):
        for step in (1, -1, 0):
            for side in (0, 1, -1):
                if step or side:
                    conditions = [c for c in (has[sign * side], z_has[sign * step]) if c is not None]
                    condition = functools.reduce(jnp.logical_and, conditions)
                    def run(side=side, step=step):
                        act(u0_copy(side, step))
                    when(condition, run)

    each_u0(lambda copy: copy.start(), 1)
    each_slab(0, slab_start)
    each_slab(1, slab_start)

    own = pl.ds(0, rows)
    u0_buf[1 : depth + 1, :, own] = guess[...]
    mat_buf[pl.ds(base, depth), own] = material[...]
    cl_buf[pl.ds(base, depth), own] = clamped[...]
    edge = jnp.zeros((comps, wide, lanes), jnp.float32)
    m_buf[0] = edge[0]
    du_buf[0] = edge
    du_buf[height + 1] = edge

    lane = lax.broadcasted_iota(jnp.int32, (wide, lanes), 1)
    row = lax.broadcasted_iota(jnp.int32, (wide, lanes), 0)
    inside_next = lane < lanes - 1
    inside_prev = lane > 0
    before_first = (row >= wide - 3) & (tile == 0)

    def y_next(a):
        return jnp.where(inside_next, pltpu.roll(a, lanes - 1, 1), 0.0)

    def y_prev(a):
        return jnp.where(inside_prev, pltpu.roll(a, 1, 1), 0.0)

    def x_next(a):
        return pltpu.roll(a, wide - 1, 0)

    def x_prev(a):
        return pltpu.roll(a, 1, 0)

    def plane_modes(u):
        out = []
        for comp in range(3):
            ahead = y_next(u[comp])
            both = (u[comp] + ahead, ahead - u[comp])
            steps = [x_next(b) for b in both]
            out.append([both[0] + steps[0], both[1] + steps[1], steps[0] - both[0], steps[1] - both[1]])
        return out

    def element(lower, upper, m):
        modes = {}
        for comp in range(3):
            for h in range(4):
                modes[h, comp] = lower[comp][h] + upper[comp][h]
                modes[4 + h, comp] = upper[comp][h] - lower[comp][h]
        force = {}
        for key, parts in terms.items():
            force[key] = m * total(modes[other] * weight for other, weight in parts) if parts else None
        low, high = [], []
        for comp in range(3):
            low.append([])
            high.append([])
            for h in range(4):
                even, odd = force[h, comp], force[4 + h, comp]
                if even is None:
                    low[comp].append(-odd)
                    high[comp].append(odd)
                elif odd is None:
                    low[comp].append(even)
                    high[comp].append(even)
                else:
                    low[comp].append(even - odd)
                    high[comp].append(even + odd)
        return low, high

    def node_force(f):
        out = []
        for comp in range(3):
            even = (f[comp][0] - f[comp][2]) + x_prev(f[comp][0] + f[comp][2])
            odd = (f[comp][1] - f[comp][3]) + x_prev(f[comp][1] + f[comp][3])
            out.append((even - odd) + y_prev(even + odd))
        return out

    def added(a, b):
        return [[p + q for p, q in zip(s, t)] for s, t in zip(a, b)]

    def planes(ref, index):
        return [ref[index, comp] for comp in range(3)]

    def layer_force(field, first, m_first, lower, held):
        upper = plane_modes(planes(field, first + 1))
        low, high = element(lower, upper, m_buf[m_first])
        return node_force(added(low, held)), upper, high

    blank = jnp.zeros((wide, lanes), jnp.float32)
    nothing = [[blank] * 4 for _ in range(3)]

    each_u0(lambda copy: copy.wait_recv(), -1)
    each_slab(0, slab_arrive)
    support, part = moduli[0], moduli[1]

    def fill_modulus(k, carry):
        m = jnp.where(mat_buf[k] == 1, part, support)
        m_buf[k + 1] = jnp.where(before_first, 0.0, m)
        return carry

    lax.fori_loop(0, height, fill_modulus, 0)

    def first_residual(k, carry):
        lower, held = carry
        force, upper, high = layer_force(u0_buf, k + 1, base + k + 1, lower, held)
        is_free = clamped[k] == 0
        for comp in range(3):
            r_buf[base + k, comp, own] = jnp.where(is_free, loads[k, comp] - force[comp][:rows], 0.0)
        return upper, high

    start = plane_modes(planes(u0_buf, 0))
    lower = plane_modes(planes(u0_buf, 1))
    unused, held = element(start, lower, m_buf[base])
    lax.fori_loop(0, depth, first_residual, (lower, held))
    each_slab(2, slab_start)
    each_slab(1, slab_arrive)

    def fill_free(k, carry):
        free_buf[k] = 1.0 - cl_buf[k].astype(jnp.float32)
        return carry

    lax.fori_loop(0, height, fill_free, 0)
    free_buf[height] = blank

    kzz, kxx, kyy = (float(stiff[c, c]) for c in range(3))
    kzx, kzy, kxy = float(stiff[0, 1]), float(stiff[0, 2]), float(stiff[1, 2])
    uzz, uxx, uyy = (float(stiff[c, 12 + c]) for c in range(3))
    uzx, uzy, uxy = -float(stiff[0, 13]), -float(stiff[0, 14]), float(stiff[1, 14])
    uxz, uyz = -float(stiff[1, 12]), -float(stiff[2, 12])
    pairs = ((0, 0), (0, 1), (0, 2), (1, 1), (1, 2), (2, 2))

    def corner_sums(m):
        behind = y_prev(m)
        plus, minus = m + behind, behind - m
        plus_b, minus_b = x_prev(plus), x_prev(minus)
        return plus + plus_b, plus_b - plus, minus + minus_b, minus_b - minus

    def factor(k, carry):
        sums_below, schur = carry
        sums = corner_sums(m_buf[k + 1])
        free = free_buf[k]
        is_free = free > 0.5
        next_free = free * free_buf[k + 1]
        s, sx, sy, sxy = [a + b for a, b in zip(sums, (sums_below[0], -sums_below[1], -sums_below[2], sums_below[3]))]
        diagonal = {
            (0, 0): jnp.where(is_free, kzz * s, 1.0), (1, 1): jnp.where(is_free, kxx * s, 1.0),
            (2, 2): jnp.where(is_free, kyy * s, 1.0), (0, 1): free * (-kzx * sx),
            (0, 2): free * (-kzy * sy), (1, 2): free * (kxy * sxy),
        }
        t, tx, ty, txy = [next_free * a for a in sums]
        up = [
            [uzz * t, uzx * tx, uzy * ty],
            [uxz * tx, uxx * t, uxy * txy],
            [uyz * ty, uxy * txy, uyy * t],
        ]
        following = []
        for shift in range(len(relax_shifts)):
            scale = 1.0 + relax_shifts[shift]
            a = {}
            for at, (p, q) in enumerate(pairs):
                d = diagonal[p, q] if scale == 1.0 else scale * diagonal[p, q]
                a[p, q] = a[q, p] = d - schur[shift][at]
            c00 = a[1, 1] * a[2, 2] - a[1, 2] * a[1, 2]
            c01 = a[1, 2] * a[0, 2] - a[0, 1] * a[2, 2]
            c02 = a[0, 1] * a[1, 2] - a[1, 1] * a[0, 2]
            c11 = a[0, 0] * a[2, 2] - a[0, 2] * a[0, 2]
            c12 = a[0, 1] * a[0, 2] - a[0, 0] * a[1, 2]
            c22 = a[0, 0] * a[1, 1] - a[0, 1] * a[0, 1]
            inverse_det = 1.0 / (a[0, 0] * c00 + a[0, 1] * c01 + a[0, 2] * c02)
            w = {}
            for at, ((p, q), c) in enumerate(zip(pairs, (c00, c01, c02, c11, c12, c22))):
                w[p, q] = w[q, p] = c * inverse_det
                fac_buf[k, shift, at] = w[p, q]
            couple = [[w[p, 0] * up[0][q] + w[p, 1] * up[1][q] + w[p, 2] * up[2][q] for q in range(3)] for p in range(3)]
            for p in range(3):
                for q in range(3):
                    fac_buf[k, shift, 6 + 3 * p + q] = couple[p][q]
            following.append([
                up[0][p] * couple[0][q] + up[1][p] * couple[1][q] + up[2][p] * couple[2][q] for p, q in pairs
            ])
        return list(sums), following

    count = len(relax_shifts)
    lax.fori_loop(0, height, factor, ([blank] * 4, [[blank] * 6 for _ in range(count)]))

    each_slab(2, slab_arrive)

    def eliminate(k, residual, y_below):
        out = []
        for shift in range(count):
            y = [residual[comp] - y_below[shift][comp] for comp in range(3)]
            for comp in range(3):
                y_buf[k, shift, comp] = y[comp]
            out.append([
                total(fac_buf[k, shift, 6 + 3 * p + q] * y[p] for p in range(3)) for q in range(3)
            ])
        return out

    no_y = [[blank] * 3 for _ in range(count)]
    spots = {pair: at for at, pair in enumerate(pairs)}

    def back(first):
        def step(i, x_above):
            k = height - 1 - i
            solved, change = [], [None] * 3
            for shift in range(count):
                y = [y_buf[k, shift, comp] for comp in range(3)]
                w = [fac_buf[k, shift, at] for at in range(6)]
                x = []
                for p in range(3):
                    own_part = total(w[spots[min(p, q), max(p, q)]] * y[q] for q in range(3))
                    above = total(fac_buf[k, shift, 6 + 3 * p + q] * x_above[shift][q] for q in range(3))
                    x.append(own_part - above)
                    term = relax_weights[shift] * x[p]
                    change[p] = term if change[p] is None else change[p] + term
                solved.append(x)
            for comp in range(3):
                du_buf[k + 1, comp] = change[comp] if first else du_buf[k + 1, comp] + change[comp]
            return solved

        lax.fori_loop(0, height, step, no_y)

    def forward_first(k, y_below):
        return eliminate(k, planes(r_buf, k), y_below)

    def forward_next(k, carry):
        lower, held, y_below = carry
        force, upper, high = layer_force(du_buf, k + 1, k + 1, lower, held)
        free = free_buf[k]
        residual = [r_buf[k, comp] - free * force[comp] for comp in range(3)]
        return upper, high, eliminate(k, residual, y_below)

    lax.fori_loop(0, height, forward_first, no_y)
    back(True)
    for sweep in range(1, SWEEPS):
        lax.fori_loop(0, height, forward_next, (plane_modes(planes(du_buf, 1)), nothing, no_y))
        back(False)

    def last_residual(k, carry):
        lower, held = carry
        force, upper, high = layer_force(du_buf, base + k + 1, base + k + 1, lower, held)
        free = free_buf[base + k, own]
        for comp in range(3):
            imbalance[k, comp] = r_buf[base + k, comp, own] - free * force[comp][:rows]
            distortion[k, comp] = guess[k, comp] + du_buf[base + k + 1, comp, own]
        return upper, high

    start = plane_modes(planes(du_buf, base))
    lower = plane_modes(planes(du_buf, base + 1))
    unused, held = element(start, lower, m_buf[base])
    lax.fori_loop(0, depth, last_residual, (lower, held))

    each_u0(lambda copy: copy.wait_send(), 1)
    for kind in range(3):
        each_slab(kind, slab_sent)


def on_device(layers, tiles, loads, guess, material, clamped, moduli):
    depth, comps, rows, lanes = loads.shape
    height, wide, count = depth * layers, 2 * rows, len(relax_shifts)
    f32, i32 = jnp.float32, jnp.int32
    vmem = pl.BlockSpec(memory_space=pltpu.VMEM)
    shape = jax.ShapeDtypeStruct(loads.shape, f32)
    return pl.pallas_call(
        functools.partial(kernel, layers, tiles),
        out_shape=(shape, shape),
        in_specs=[vmem] * 4 + [pl.BlockSpec(memory_space=pltpu.SMEM)],
        out_specs=(vmem, vmem),
        scratch_shapes=[
            pltpu.VMEM((height, wide, lanes), i32),
            pltpu.VMEM((height, wide, lanes), i32),
            pltpu.VMEM((depth + 2, comps, wide, lanes), f32),
            pltpu.VMEM((height, comps, wide, lanes), f32),
            pltpu.VMEM((height + 1, wide, lanes), f32),
            pltpu.VMEM((height + 1, wide, lanes), f32),
            pltpu.VMEM((height + 2, comps, wide, lanes), f32),
            pltpu.VMEM((height, count, 15, wide, lanes), f32),
            pltpu.VMEM((height, count, comps, wide, lanes), f32),
            pltpu.SemaphoreType.DMA((3, 3, layers)),
            pltpu.SemaphoreType.DMA((3, 3, layers)),
            pltpu.SemaphoreType.DMA((3, 3)),
            pltpu.SemaphoreType.DMA((3, 3)),
        ],
        compiler_params=pltpu.CompilerParams(
            collective_id=0, has_side_effects=True, vmem_limit_bytes=40 * 1024 * 1024
        ),
        name="relax",
    )(loads, guess, material, clamped, moduli)


def solution(mesh):
    field, plane = P("build", None, "tile", None), P("build", "tile", None)
    return jax.shard_map(
        functools.partial(on_device, mesh.shape["build"], mesh.shape["tile"]),
        mesh=mesh,
        in_specs=(field, field, plane, plane, P()),
        out_specs=(field, field),
        check_vma=False,
    )
```
